256 devices in a mesh: clip: 2 (over y_lo), patch: 16 (over z, core), frame: 8 (over y_hi, x).
Axes of the slice: x: 4, y: 4 (y_hi: 2, y_lo: 2; y = y_hi * 2 + y_lo), z: 8, core: 2. Of those that a mesh axis runs over, the one named last changes fastest.
Arguments:
- queries: bfloat16 [4, 16, 1024, 2048], P('clip', 'frame', 'patch'), may hold values from -48 to 48, as said below
- keys: bfloat16 [4, 16, 1024, 2048], P('clip', 'frame', 'patch'), may hold values from -48 to 48, as said below
- values: bfloat16 [4, 16, 1024, 2048], P('clip', 'frame', 'patch'), may hold values from -6 to 6
- grad_out: bfloat16 [4, 16, 1024, 2048], P('clip', 'frame', 'patch'), may hold values from -6 to 6
- gain_q: float32 [16, 128], P('patch'), may hold values from 0.5 to 5.5, as said below
- gain_k: float32 [16, 128], P('patch'), may hold values from 0.5 to 5.5, as said below
Outputs:
- grad_queries: bfloat16 [4, 16, 1024, 2048], P('clip', 'frame', 'patch')
- grad_keys: bfloat16 [4, 16, 1024, 2048], P('clip', 'frame', 'patch')
- grad_values: bfloat16 [4, 16, 1024, 2048], P('clip', 'frame', 'patch')
- gain_grads: float32 [2, 16, 128], P(None, 'patch')
The draws below stay inside these ranges and needn't reach their ends.
Inputs may be any that keep to these rules, and one draw needn't show every extreme that they name: `queries`: finite real values. `keys`: finite real values. `gain_q`: positive gains. `gain_k`: positive gains.
All inputs are finite; a program needn't handle non-finite values.
Results may differ from the reference program's by a relative error of at most 0.034.
The reference program's roundings to bfloat16 on the way (of `q_norm`, `prob_low` and `dscore`) count: a program that leaves them out, or rounds other values in their place, can miss the bound.
Values may be sent and summed in bfloat16 or wider, within the bound.
No kernel may reach another device: no remote copies, remote signals or barrier semaphores. Data moves between devices by JAX's collectives and lax.ppermute only.
A program may use at most 128 MiB of HBM per device.

```python
import math
import jax
import jax.numpy as jnp
from jax import lax

HEAD_DIM = 128
HEADS = 16
WIDTH = 2048
FRAMES = 16
CLIPS = 4
PATCHES = 1024


def field_parts(key):
    shape = (CLIPS, FRAMES, PATCHES, HEADS, HEAD_DIM)
    parts = jax.random.split(key, 5)
    base_q = jax.random.truncated_normal(parts[0], -4.0, 4.0, shape, jnp.float32)
    base_k = jax.random.truncated_normal(parts[1], -4.0, 4.0, shape, jnp.float32)
    low = math.log(0.3)
    high = math.log(3.0)
    rows_q = jnp.exp(jax.random.uniform(parts[2], shape[:4] + (1,), jnp.float32, low, high))
    rows_k = jnp.exp(jax.random.uniform(parts[3], shape[:4] + (1,), jnp.float32, low, high))
    columns = jnp.exp(jax.random.uniform(parts[4], (HEADS, HEAD_DIM), jnp.float32, low, high))
    return (base_q * rows_q * columns, base_k * rows_k * columns)


def draw_queries(key, part):
    drawn_q, drawn_k = field_parts(key)
    return drawn_q.reshape(CLIPS, FRAMES, PATCHES, HEADS * HEAD_DIM).astype(jnp.bfloat16)


def draw_keys(key, part):
    drawn_q, drawn_k = field_parts(key)
    return drawn_k.reshape(CLIPS, FRAMES, PATCHES, HEADS * HEAD_DIM).astype(jnp.bfloat16)


def draw_gain_q(key, part):
    key = jax.random.fold_in(key, 31)
    second = jax.random.fold_in(key, 1)
    return jax.random.uniform(second, (HEADS, HEAD_DIM), jnp.float32, 0.7, 1.3)


def draw_gain_k(key, part):
    key = jax.random.fold_in(key, 47)
    second = jax.random.fold_in(key, 1)
    return jax.random.uniform(second, (HEADS, HEAD_DIM), jnp.float32, 0.7, 1.3)


def levels(own_key, dims, shards, low, high):
    level = 1.0
    for dim, blocks in shards:
        heights = jax.random.uniform(jax.random.fold_in(jax.random.fold_in(own_key, 6), dim), (blocks,), jnp.float32, low / len(shards), high / len(shards))
        level = level * jnp.repeat(jnp.exp(heights), dims[dim] // blocks).reshape((-1,) + (1,) * (len(dims) - 1 - dim))
    return level


def bell_draw(own_key, extent, width, bound, pieces=(), kind=jnp.bfloat16):
    factor_of = levels(own_key, extent, pieces, -0.22, 0.18) if pieces else 1.0
    result = jax.random.normal(own_key, extent, jnp.float32) * width * factor_of
    return jnp.minimum(jnp.maximum(result, -bound), bound).astype(kind)


def setup_inputs(seed: int = 0) -> dict:
    key_of = jax.random.split(jax.random.key(seed), 7)
    return {
        "queries": draw_queries(jax.random.fold_in(key_of[6], 71), 0),
        "keys": draw_keys(jax.random.fold_in(key_of[6], 71), 0),
        "values": bell_draw(key_of[2], (CLIPS, FRAMES, PATCHES, WIDTH), 1.0, 6.0, ((0, 2), (1, 8), (2, 16))),
        "grad_out": bell_draw(key_of[3], (CLIPS, FRAMES, PATCHES, WIDTH), 1.0, 6.0, ((0, 2), (1, 8), (2, 16))),
        "gain_q": draw_gain_q(jax.random.fold_in(key_of[6], 71), 0),
        "gain_k": draw_gain_k(jax.random.fold_in(key_of[6], 71), 0),
    }


EPS = 1e-06

def normalize(raw, gain):
    wide = raw.astype(jnp.float32)
    scale = lax.rsqrt(lax.optimization_barrier(jnp.mean(wide * wide, axis=-1, keepdims=True)) + EPS)
    unit = wide * scale
    return (unit, scale, lax.optimization_barrier((unit * gain).astype(jnp.bfloat16)))

def restore(grad_norm, unit, scale, gain):
    grad_unit = grad_norm * gain
    along = lax.optimization_barrier(jnp.mean(grad_unit * unit, axis=-1, keepdims=True))
    return ((scale * (grad_unit - unit * along)).astype(jnp.bfloat16), grad_norm * unit)

def frame_grads(items, gain_q, gain_k):
    queries, keys, values, grad_out = items
    wide = jnp.float32
    inverse = 1.0 / math.sqrt(HEAD_DIM)
    q_unit, q_scale, q_norm = normalize(queries, gain_q)
    k_unit, k_scale, k_norm = normalize(keys, gain_k)
    scores = jnp.einsum('phe,khe->hpk', q_norm.astype(wide), k_norm.astype(wide)) * inverse
    top = lax.optimization_barrier(jnp.max(scores, axis=-1, keepdims=True))
    expo = jnp.exp(scores - top)
    prob = expo / lax.optimization_barrier(jnp.sum(expo, axis=-1, keepdims=True))
    prob_low = lax.optimization_barrier(prob.astype(jnp.bfloat16))
    dprob = jnp.einsum('phe,khe->hpk', grad_out.astype(wide), values.astype(wide))
    delta = lax.optimization_barrier(jnp.sum(prob * dprob, axis=-1, keepdims=True))
    dscore = lax.optimization_barrier((prob * (dprob - delta)).astype(jnp.bfloat16))
    grad_v = jnp.einsum('hpk,phe->khe', prob_low.astype(wide), grad_out.astype(wide)).astype(jnp.bfloat16)
    grad_qn = jnp.einsum('hpk,khe->phe', dscore.astype(wide), k_norm.astype(wide)) * inverse
    grad_kn = jnp.einsum('hpk,phe->khe', dscore.astype(wide), q_norm.astype(wide)) * inverse
    grad_q, term_q = restore(grad_qn, q_unit, q_scale, gain_q)
    grad_k, term_k = restore(grad_kn, k_unit, k_scale, gain_k)
    return (grad_q, grad_k, grad_v, lax.optimization_barrier(jnp.sum(term_q, axis=0)), lax.optimization_barrier(jnp.sum(term_k, axis=0)))

def reference(queries, keys, values, grad_out, gain_q, gain_k):
    split_shape = (CLIPS * FRAMES, PATCHES, HEADS, HEAD_DIM)
    items = tuple((a.reshape(split_shape) for a in (queries, keys, values, grad_out)))
    gq = gain_q.astype(jnp.float32)
    gk = gain_k.astype(jnp.float32)
    grad_q, grad_k, grad_v, term_q, term_k = lax.map(lambda it: frame_grads(it, gq, gk), items)
    full_shape = (CLIPS, FRAMES, PATCHES, HEADS * HEAD_DIM)
    gain_grads = jnp.stack([lax.optimization_barrier(jnp.sum(term_q, axis=0)), lax.optimization_barrier(jnp.sum(term_k, axis=0))])
    return (grad_q.reshape(full_shape), grad_k.reshape(full_shape), grad_v.reshape(full_shape), gain_grads)
```

```python
import functools
import math

import jax
import jax.numpy as jnp
from jax import lax
from jax.experimental import pallas as pl
from jax.experimental.pallas import tpu as pltpu
from jax.sharding import PartitionSpec as P

EPS = 1e-06
HEADS = 16
DEPTH = 128
BLOCK = 256
CHUNKS = ((0, 1), (1, 2))
F32 = jnp.float32
BF16 = jnp.bfloat16


def pack_kernel(q_ref, k_ref, v_ref, g_ref, out_ref):
    for a, ref in enumerate((q_ref, k_ref, v_ref, g_ref)):
        for h in range(HEADS):
            out_ref[h, a, 0] = ref[0, 0, :, h * DEPTH : (h + 1) * DEPTH]


def pack(arrays, first, clips):
    _, frames, rows, width = arrays[0].shape
    items = clips * frames
    spec = pl.BlockSpec((1, 1, rows, width), lambda i: (first + i // frames, i % frames, 0, 0))
    return pl.pallas_call(
        pack_kernel,
        grid=(items,),
        in_specs=[spec] * 4,
        out_specs=pl.BlockSpec((HEADS, 4, 1, rows, DEPTH), lambda i: (0, 0, i, 0, 0)),
        out_shape=jax.ShapeDtypeStruct((HEADS, 4, items, rows, DEPTH), BF16),
        name="pack",
    )(*arrays)


def unpack_kernel(in_ref, *refs):
    for a, ref in enumerate(refs[-3:]):
        for h in range(HEADS):
            ref[0, 0, :, h * DEPTH : (h + 1) * DEPTH] = in_ref[h, a, 0]


def unpack(arrived, first, clips, shape, earlier):
    _, frames, rows, width = shape
    items = clips * frames
    spec = pl.BlockSpec((1, 1, rows, width), lambda i: (first + i // frames, i % frames, 0, 0))
    return pl.pallas_call(
        unpack_kernel,
        grid=(items,),
        in_specs=[pl.BlockSpec((HEADS, 3, 1, rows, DEPTH), lambda i: (0, 0, i, 0, 0))]
        + [pl.BlockSpec(memory_space=pl.ANY)] * len(earlier),
        out_specs=[spec] * 3,
        out_shape=[jax.ShapeDtypeStruct(shape, BF16)] * 3,
        input_output_aliases={1 + i: i for i in range(len(earlier))},
        name="unpack",
    )(arrived, *earlier)


def normalize(raw, gain):
    wide = raw.astype(F32)
    scale = lax.rsqrt(jnp.mean(wide * wide, axis=-1, keepdims=True) + EPS)
    unit = wide * scale
    return unit, scale, (unit * gain).astype(BF16)


def restore(grad_norm, unit, scale, gain):
    grad_unit = grad_norm * gain
    along = jnp.mean(grad_unit * unit, axis=-1, keepdims=True)
    return (scale * (grad_unit - unit * along)).astype(BF16), grad_norm * unit


def dot(a, b, dims):
    return lax.dot_general(a, b, (dims, ((), ())), preferred_element_type=F32)


def attend_kernel(in_ref, gain_q_ref, gain_k_ref, out_ref, gains_ref, gv_ref, gk_ref):
    sources, _, _, rows, depth = in_ref.shape
    total = sources * rows
    inverse = 1.0 / math.sqrt(depth)
    gain_q = gain_q_ref[...]
    gain_k = gain_k_ref[...]

    def whole(a):
        return in_ref[:, a, 0].reshape(total, depth)

    k_unit, k_scale, k_norm = normalize(whole(1), gain_k)
    values = whole(2)
    k_turned = k_norm.T
    each = BLOCK // rows
    term_q = jnp.zeros((1, depth), F32)
    for b in range(total // BLOCK):
        part = pl.ds(b * each, each)
        q_unit, q_scale, q_norm = normalize(in_ref[part, 0, 0].reshape(BLOCK, depth), gain_q)
        grad_out = in_ref[part, 3, 0].reshape(BLOCK, depth)
        scores = dot(k_norm, q_norm, ((1,), (1,)))
        top = jnp.max(scores, axis=0, keepdims=True)
        expo = jnp.exp((scores - top) * inverse)
        prob = expo * (1.0 / jnp.sum(expo, axis=0, keepdims=True))
        dprob = dot(values, grad_out, ((1,), (1,)))
        delta = jnp.sum(prob * dprob, axis=0, keepdims=True)
        dscore = (prob * (dprob - delta)).astype(BF16)
        grad_v = dot(prob.astype(BF16), grad_out, ((1,), (0,)))
        grad_k = dot(dscore, q_norm, ((1,), (0,)))
        if b == 0:
            gv_ref[...] = grad_v
            gk_ref[...] = grad_k
        else:
            gv_ref[...] += grad_v
            gk_ref[...] += grad_k
        grad_qn = dot(k_turned, dscore, ((1,), (0,))).T * inverse
        grad_q, term = restore(grad_qn, q_unit, q_scale, gain_q)
        out_ref[part, 0, 0] = grad_q.reshape(each, rows, depth)
        term_q += jnp.sum(term, axis=0, keepdims=True)
    grad_k, term = restore(gk_ref[...] * inverse, k_unit, k_scale, gain_k)
    out_ref[:, 1, 0] = grad_k.reshape(sources, rows, depth)
    out_ref[:, 2, 0] = gv_ref[...].astype(BF16).reshape(sources, rows, depth)
    gains_ref[0, 0:1] = term_q
    gains_ref[0, 1:2] = jnp.sum(term, axis=0, keepdims=True)


def attend(arrived, gain_q, gain_k):
    sources, _, items, rows, depth = arrived.shape
    total = sources * rows
    gain = pl.BlockSpec((1, depth), lambda i: (0, 0))
    return pl.pallas_call(
        attend_kernel,
        grid=(items,),
        in_specs=[
            pl.BlockSpec((sources, 4, 1, rows, depth), lambda i: (0, 0, i, 0, 0)),
            gain,
            gain,
        ],
        out_specs=[
            pl.BlockSpec((sources, 3, 1, rows, depth), lambda i: (0, 0, i, 0, 0)),
            pl.BlockSpec((1, 2, depth), lambda i: (i, 0, 0)),
        ],
        out_shape=[
            jax.ShapeDtypeStruct((sources, 3, items, rows, depth), BF16),
            jax.ShapeDtypeStruct((items, 2, depth), F32),
        ],
        scratch_shapes=[pltpu.VMEM((total, depth), F32)] * 2,
        compiler_params=pltpu.CompilerParams(vmem_limit_bytes=40 * 1024 * 1024),
        cost_estimate=pl.CostEstimate(
            flops=items * 10 * total * total * depth,
            bytes_accessed=items * total * depth * 14,
            transcendentals=items * total * total,
        ),
        name="attend",
    )(arrived, gain_q, gain_k)


def body(queries, keys, values, grad_out, gain_q, gain_k):
    arrays = (queries, keys, values, grad_out)
    exchange = functools.partial(
        lax.all_to_all, axis_name="patch", split_axis=0, concat_axis=0, tiled=True
    )
    arrived = [exchange(pack(arrays, first, last - first)) for first, last in CHUNKS]
    done = [attend(a, gain_q, gain_k) for a in arrived]
    grads = ()
    for (first, last), (leaving, _) in zip(CHUNKS, done):
        grads = unpack(exchange(leaving), first, last - first, queries.shape, grads)
    terms = sum(jnp.sum(gains, axis=0) for _, gains in done)
    gain_grads = lax.psum(terms, ("clip", "frame")).reshape(2, 1, DEPTH)
    return (*grads, gain_grads)


def solution(mesh):
    wide = P("clip", "frame", "patch", None)
    gain = P("patch", None)
    return jax.shard_map(
        body,
        mesh=mesh,
        in_specs=(wide, wide, wide, wide, gain, gain),
        out_specs=(wide, wide, wide, P(None, "patch", None)),
        check_vma=False,
    )
```

```python
import functools
import math

import jax
import jax.numpy as jnp
from jax import lax
from jax.experimental import pallas as pl
from jax.experimental.pallas import tpu as pltpu
from jax.sharding import PartitionSpec as P

EPS = 1e-06
HEADS = 16
DEPTH = 128
BLOCK = 256
VMEM_LIMIT = 63 * 1024 * 1024
CHUNKS = ((0, 1), (1, 2))
F32 = jnp.float32
BF16 = jnp.bfloat16


def pack_kernel(q_ref, k_ref, v_ref, g_ref, out_ref):
    for a, ref in enumerate((q_ref, k_ref, v_ref, g_ref)):
        for h in range(HEADS):
            out_ref[h, a, 0] = ref[0, 0, :, h * DEPTH : (h + 1) * DEPTH]


def pack(arrays, first, clips):
    _, frames, rows, width = arrays[0].shape
    items = clips * frames
    spec = pl.BlockSpec((1, 1, rows, width), lambda i: (first + i // frames, i % frames, 0, 0))
    return pl.pallas_call(
        pack_kernel,
        grid=(items,),
        in_specs=[spec] * 4,
        out_specs=pl.BlockSpec((HEADS, 4, 1, rows, DEPTH), lambda i: (0, 0, i, 0, 0)),
        out_shape=jax.ShapeDtypeStruct((HEADS, 4, items, rows, DEPTH), BF16),
        compiler_params=pltpu.CompilerParams(vmem_limit_bytes=VMEM_LIMIT),
        name="pack",
    )(*arrays)


def unpack_kernel(in_ref, *refs):
    for a, ref in enumerate(refs[-3:]):
        for h in range(HEADS):
            ref[0, 0, :, h * DEPTH : (h + 1) * DEPTH] = in_ref[h, a, 0]


def unpack(arrived, first, clips, shape, earlier):
    _, frames, rows, width = shape
    items = clips * frames
    spec = pl.BlockSpec((1, 1, rows, width), lambda i: (first + i // frames, i % frames, 0, 0))
    return pl.pallas_call(
        unpack_kernel,
        grid=(items,),
        in_specs=[pl.BlockSpec((HEADS, 3, 1, rows, DEPTH), lambda i: (0, 0, i, 0, 0))]
        + [pl.BlockSpec(memory_space=pl.ANY)] * len(earlier),
        out_specs=[spec] * 3,
        out_shape=[jax.ShapeDtypeStruct(shape, BF16)] * 3,
        input_output_aliases={1 + i: i for i in range(len(earlier))},
        compiler_params=pltpu.CompilerParams(vmem_limit_bytes=VMEM_LIMIT),
        name="unpack",
    )(arrived, *earlier)


def normalize(raw, gain):
    wide = raw.astype(F32)
    scale = lax.rsqrt(jnp.mean(wide * wide, axis=-1, keepdims=True) + EPS)
    unit = wide * scale
    return unit, scale, (unit * gain).astype(BF16)


def restore(grad_norm, unit, scale, gain):
    grad_unit = grad_norm * gain
    along = jnp.mean(grad_unit * unit, axis=-1, keepdims=True)
    return (scale * (grad_unit - unit * along)).astype(BF16), grad_norm * unit


def dot(a, b, dims):
    return lax.dot_general(a, b, (dims, ((), ())), preferred_element_type=F32)


def attend_kernel(in_ref, gain_q_ref, gain_k_ref, out_ref, gains_ref, gv_ref, gk_ref):
    sources, _, _, rows, depth = in_ref.shape
    total = sources * rows
    inverse = 1.0 / math.sqrt(depth)
    gain_q = gain_q_ref[...]
    gain_k = gain_k_ref[...]

    def whole(a):
        return in_ref[:, a, 0].reshape(total, depth)

    k_unit, k_scale, k_norm = normalize(whole(1), gain_k)
    values = whole(2)
    k_turned = k_norm.T
    each = BLOCK // rows
    term_q = jnp.zeros((1, depth), F32)
    for b in range(total // BLOCK):
        part = pl.ds(b * each, each)
        q_unit, q_scale, q_norm = normalize(in_ref[part, 0, 0].reshape(BLOCK, depth), gain_q)
        grad_out = in_ref[part, 3, 0].reshape(BLOCK, depth)
        scores = dot(k_norm, q_norm, ((1,), (1,)))
        top = jnp.max(scores, axis=0, keepdims=True)
        expo = jnp.exp2((scores - top) * (inverse * math.log2(math.e)))
        prob = expo * (1.0 / jnp.sum(expo, axis=0, keepdims=True))
        dprob = dot(values, grad_out, ((1,), (1,)))
        delta = jnp.sum(prob * dprob, axis=0, keepdims=True)
        dscore = (prob * (dprob - delta)).astype(BF16)
        grad_v = dot(prob.astype(BF16), grad_out, ((1,), (0,)))
        grad_k = dot(dscore, q_norm, ((1,), (0,)))
        if b == 0:
            gv_ref[...] = grad_v
            gk_ref[...] = grad_k
        else:
            gv_ref[...] += grad_v
            gk_ref[...] += grad_k
        grad_qn = dot(k_turned, dscore, ((1,), (0,))).T * inverse
        grad_q, term = restore(grad_qn, q_unit, q_scale, gain_q)
        out_ref[part, 0, 0] = grad_q.reshape(each, rows, depth)
        term_q += jnp.sum(term, axis=0, keepdims=True)
    grad_k, term = restore(gk_ref[...] * inverse, k_unit, k_scale, gain_k)
    out_ref[:, 1, 0] = grad_k.reshape(sources, rows, depth)
    out_ref[:, 2, 0] = gv_ref[...].astype(BF16).reshape(sources, rows, depth)
    gains_ref[0, 0:1] = term_q
    gains_ref[0, 1:2] = jnp.sum(term, axis=0, keepdims=True)


def attend(arrived, gain_q, gain_k):
    sources, _, items, rows, depth = arrived.shape
    total = sources * rows
    gain = pl.BlockSpec((1, depth), lambda i: (0, 0))
    return pl.pallas_call(
        attend_kernel,
        grid=(items,),
        in_specs=[
            pl.BlockSpec((sources, 4, 1, rows, depth), lambda i: (0, 0, i, 0, 0)),
            gain,
            gain,
        ],
        out_specs=[
            pl.BlockSpec((sources, 3, 1, rows, depth), lambda i: (0, 0, i, 0, 0)),
            pl.BlockSpec((1, 2, depth), lambda i: (i, 0, 0)),
        ],
        out_shape=[
            jax.ShapeDtypeStruct((sources, 3, items, rows, depth), BF16),
            jax.ShapeDtypeStruct((items, 2, depth), F32),
        ],
        scratch_shapes=[pltpu.VMEM((total, depth), F32)] * 2,
        compiler_params=pltpu.CompilerParams(vmem_limit_bytes=VMEM_LIMIT),
        cost_estimate=pl.CostEstimate(
            flops=items * 10 * total * total * depth,
            bytes_accessed=items * total * depth * 14,
            transcendentals=items * total * total,
        ),
        name="attend",
    )(arrived, gain_q, gain_k)


def total_of(x):
    for axis in ("clip", "frame"):
        size, step = lax.axis_size(axis), 1
        while step < size:
            x = x + lax.ppermute(x, axis, [(i, i ^ step) for i in range(size)])
            step *= 2
    return x


def body(queries, keys, values, grad_out, gain_q, gain_k):
    arrays = (queries, keys, values, grad_out)
    exchange = functools.partial(
        lax.all_to_all, axis_name="patch", split_axis=0, concat_axis=0, tiled=True
    )
    arrived = [exchange(pack(arrays, first, last - first)) for first, last in CHUNKS]
    done = [attend(a, gain_q, gain_k) for a in arrived]
    grads = ()
    for (first, last), (leaving, _) in zip(CHUNKS, done):
        grads = unpack(exchange(leaving), first, last - first, queries.shape, grads)
    terms = sum(jnp.sum(gains, axis=0) for _, gains in done)
    gain_grads = total_of(terms).reshape(2, 1, DEPTH)
    return (*grads, gain_grads)


def solution(mesh):
    wide = P("clip", "frame", "patch", None)
    gain = P("patch", None)
    return jax.shard_map(
        body,
        mesh=mesh,
        in_specs=(wide, wide, wide, wide, gain, gain),
        out_specs=(wide, wide, wide, P(None, "patch", None)),
        check_vma=False,
    )
```

```python
import math

import jax
import jax.numpy as jnp
from jax import lax
from jax.experimental import pallas as pl
from jax.experimental.pallas import tpu as pltpu
from jax.sharding import PartitionSpec as P

EPS = 1e-06
HEADS = 16
DEPTH = 128
BLOCK = 256
VMEM_LIMIT = 63 * 1024 * 1024
WINDOW = 4
CHIPS = HEADS // 2
ORDER = (1, 7, 2, 6, 3, 5, 4)
F32 = jnp.float32
BF16 = jnp.bfloat16


def partner(index, slot):
    z, core = index // 2, index % 2
    return (z + (slot if core == 0 else CHIPS - slot)) % CHIPS * 2 + core


def chip_of(index, slot):
    return ((index >> 1) + jnp.where((index & 1) == 0, slot, CHIPS - slot)) & (CHIPS - 1)


def source_of(index, slot):
    return chip_of(index, CHIPS - slot)


def pack_kernel(q_ref, k_ref, v_ref, g_ref, out_ref):
    for a, ref in enumerate((q_ref, k_ref, v_ref, g_ref)):
        for h in range(HEADS):
            out_ref[h, a, 0] = ref[0, 0, :, h * DEPTH : (h + 1) * DEPTH]


def pack(arrays, first, clips):
    _, frames, rows, width = arrays[0].shape
    items = clips * frames
    spec = pl.BlockSpec((1, 1, rows, width), lambda i: (first + i // frames, i % frames, 0, 0))
    return pl.pallas_call(
        pack_kernel,
        grid=(items,),
        in_specs=[spec] * 4,
        out_specs=pl.BlockSpec((HEADS, 4, 1, rows, DEPTH), lambda i: (0, 0, i, 0, 0)),
        out_shape=jax.ShapeDtypeStruct((HEADS, 4, items, rows, DEPTH), BF16),
        compiler_params=pltpu.CompilerParams(vmem_limit_bytes=VMEM_LIMIT),
        name="pack",
    )(*arrays)


def compose(index, own, other):
    _, kinds, items, rows, _ = own.shape

    def kernel(index_ref, own_ref, other_ref, *messages):
        for s in range(CHIPS):
            chip = chip_of(index_ref[0], s)
            messages[s][0] = own_ref[chip]
            messages[s][1] = other_ref[chip]

    return pl.pallas_call(
        kernel,
        grid_spec=pltpu.PrefetchScalarGridSpec(
            num_scalar_prefetch=1,
            grid=(items,),
            in_specs=[pl.BlockSpec((CHIPS, kinds, 1, rows, DEPTH), lambda i, _: (0, 0, i, 0, 0))] * 2,
            out_specs=[pl.BlockSpec((2, kinds, 1, rows, DEPTH), lambda i, _: (0, 0, i, 0, 0))] * CHIPS,
        ),
        out_shape=[jax.ShapeDtypeStruct((2, kinds, items, rows, DEPTH), BF16)] * CHIPS,
        compiler_params=pltpu.CompilerParams(vmem_limit_bytes=VMEM_LIMIT),
        name="compose",
    )(index, own, other)


def unpack_kernel(in_ref, *refs):
    for a, ref in enumerate(refs[-3:]):
        for h in range(HEADS):
            ref[0, 0, :, h * DEPTH : (h + 1) * DEPTH] = in_ref[h, a, 0]


def unpack_whole(arrived, first, clips, shape, earlier):
    _, frames, rows, width = shape
    items = clips * frames
    spec = pl.BlockSpec((1, 1, rows, width), lambda i: (first + i // frames, i % frames, 0, 0))
    return pl.pallas_call(
        unpack_kernel,
        grid=(items,),
        in_specs=[pl.BlockSpec((HEADS, 3, 1, rows, DEPTH), lambda i: (0, 0, i, 0, 0))]
        + [pl.BlockSpec(memory_space=pl.ANY)] * len(earlier),
        out_specs=[spec] * 3,
        out_shape=[jax.ShapeDtypeStruct(shape, BF16)] * 3,
        input_output_aliases={1 + i: i for i in range(len(earlier))},
        compiler_params=pltpu.CompilerParams(vmem_limit_bytes=VMEM_LIMIT),
        name="unpack_whole",
    )(arrived, *earlier)


def unpack(index, messages, clip, shape, earlier):
    _, frames, rows, width = shape

    def kernel(index_ref, *refs):
        for s in range(CHIPS):
            chip = source_of(index_ref[0], s)
            for hh in range(2):
                head = 2 * chip + ((index_ref[0] & 1) ^ hh)
                at = pl.ds(pl.multiple_of(head * DEPTH, DEPTH), DEPTH)
                for a in range(3):
                    refs[-3 + a][0, 0, :, at] = refs[s][hh, a, 0]

    return pl.pallas_call(
        kernel,
        grid_spec=pltpu.PrefetchScalarGridSpec(
            num_scalar_prefetch=1,
            grid=(frames,),
            in_specs=[pl.BlockSpec((2, 3, 1, rows, DEPTH), lambda i, _: (0, 0, i, 0, 0))] * CHIPS
            + [pl.BlockSpec(memory_space=pl.ANY)] * len(earlier),
            out_specs=[pl.BlockSpec((1, 1, rows, width), lambda i, _: (clip, i, 0, 0))] * 3,
        ),
        out_shape=[jax.ShapeDtypeStruct(shape, BF16)] * 3,
        input_output_aliases={1 + CHIPS + i: i for i in range(len(earlier))},
        compiler_params=pltpu.CompilerParams(vmem_limit_bytes=VMEM_LIMIT),
        name="unpack",
    )(index, *messages, *earlier)


def normalize(raw, gain):
    wide = raw.astype(F32)
    scale = lax.rsqrt(jnp.mean(wide * wide, axis=-1, keepdims=True) + EPS)
    unit = wide * scale
    return unit, scale, (unit * gain).astype(BF16)


def restore(grad_norm, unit, scale, gain):
    grad_unit = grad_norm * gain
    along = jnp.mean(grad_unit * unit, axis=-1, keepdims=True)
    return (scale * (grad_unit - unit * along)).astype(BF16), grad_norm * unit


def dot(a, b, dims):
    return lax.dot_general(a, b, (dims, ((), ())), preferred_element_type=F32)


def attend_kernel(index_ref, in_ref, gain_q_ref, gain_k_ref, *refs):
    *outs, gains_ref, gv_ref, gk_ref = refs
    sources, _, _, rows, depth = in_ref.shape
    total = sources * rows
    inverse = 1.0 / math.sqrt(depth)
    gain_q = gain_q_ref[...]
    gain_k = gain_k_ref[...]

    low = (index_ref[0] & 1) == 0

    def whole(a):
        return in_ref[:, a, 0].reshape(total, depth)

    def put(first, a, value):
        value = value.reshape(-1, 2, rows, depth)
        chips = pl.ds(first, value.shape[0])
        if len(outs) == 1:
            outs[0][chips, :, a, 0] = value
        else:
            outs[0][chips, a, 0] = jnp.where(low, value[:, 0], value[:, 1])
            outs[1][chips, a, 0] = jnp.where(low, value[:, 1], value[:, 0])

    k_unit, k_scale, k_norm = normalize(whole(1), gain_k)
    values = whole(2)
    k_turned = k_norm.T
    each = BLOCK // rows
    term_q = jnp.zeros((1, depth), F32)
    for b in range(total // BLOCK):
        part = pl.ds(b * each, each)
        q_unit, q_scale, q_norm = normalize(in_ref[part, 0, 0].reshape(BLOCK, depth), gain_q)
        grad_out = in_ref[part, 3, 0].reshape(BLOCK, depth)
        scores = dot(k_norm, q_norm, ((1,), (1,)))
        top = jnp.max(scores, axis=0, keepdims=True)
        expo = jnp.exp2((scores - top) * (inverse * math.log2(math.e)))
        prob = expo * (1.0 / jnp.sum(expo, axis=0, keepdims=True))
        dprob = dot(values, grad_out, ((1,), (1,)))
        delta = jnp.sum(prob * dprob, axis=0, keepdims=True)
        dscore = (prob * (dprob - delta)).astype(BF16)
        grad_v = dot(prob.astype(BF16), grad_out, ((1,), (0,)))
        grad_k = dot(dscore, q_norm, ((1,), (0,)))
        if b == 0:
            gv_ref[...] = grad_v
            gk_ref[...] = grad_k
        else:
            gv_ref[...] += grad_v
            gk_ref[...] += grad_k
        grad_qn = dot(k_turned, dscore, ((1,), (0,))).T * inverse
        grad_q, term = restore(grad_qn, q_unit, q_scale, gain_q)
        put(b * each // 2, 0, grad_q)
        term_q += jnp.sum(term, axis=0, keepdims=True)
    grad_k, term = restore(gk_ref[...] * inverse, k_unit, k_scale, gain_k)
    put(0, 1, grad_k)
    put(0, 2, gv_ref[...].astype(BF16))
    gains_ref[0, 0:1] = term_q
    gains_ref[0, 1:2] = jnp.sum(term, axis=0, keepdims=True)


def attend(index, arrived, gain_q, gain_k, apart):
    sources, _, items, rows, depth = arrived.shape
    total = sources * rows
    gain = pl.BlockSpec((1, depth), lambda i, _: (0, 0))
    if apart:
        outs = [(CHIPS, 3, items, rows, depth)] * 2
        specs = [pl.BlockSpec((CHIPS, 3, 1, rows, depth), lambda i, _: (0, 0, i, 0, 0))] * 2
    else:
        outs = [(CHIPS, 2, 3, items, rows, depth)]
        specs = [pl.BlockSpec((CHIPS, 2, 3, 1, rows, depth), lambda i, _: (0, 0, 0, i, 0, 0))]
    return pl.pallas_call(
        attend_kernel,
        grid_spec=pltpu.PrefetchScalarGridSpec(
            num_scalar_prefetch=1,
            grid=(items,),
            in_specs=[
                pl.BlockSpec((sources, 4, 1, rows, depth), lambda i, _: (0, 0, i, 0, 0)),
                gain,
                gain,
            ],
            out_specs=specs + [pl.BlockSpec((1, 2, depth), lambda i, _: (i, 0, 0))],
            scratch_shapes=[pltpu.VMEM((total, depth), F32)] * 2,
        ),
        out_shape=[jax.ShapeDtypeStruct(shape, BF16) for shape in outs]
        + [jax.ShapeDtypeStruct((items, 2, depth), F32)],
        compiler_params=pltpu.CompilerParams(vmem_limit_bytes=VMEM_LIMIT),
        cost_estimate=pl.CostEstimate(
            flops=items * 10 * total * total * depth,
            bytes_accessed=items * total * depth * 14,
            transcendentals=items * total * total,
        ),
        name="attend",
    )(index, arrived, gain_q, gain_k)


def totals_of(x):
    steps = []
    for axis in ("clip", "frame"):
        size, step = lax.axis_size(axis), 1
        while step < size:
            x = x + lax.ppermute(x, axis, [(i, i ^ step) for i in range(size)])
            steps.append(x)
            step *= 2
    return steps


def after(x, *earlier):
    return lax.optimization_barrier((x, *earlier))[0] if earlier else x


def swap(x):
    return lax.ppermute(x, "patch", [(i, i ^ 1) for i in range(HEADS)])


def exchange(x):
    return lax.all_to_all(x, "patch", split_axis=0, concat_axis=0, tiled=True)


def send(messages, earlier):
    landed = list(messages)
    for i, slot in enumerate(ORDER):
        before = (landed[ORDER[i - WINDOW]],) if i >= WINDOW else (earlier,)
        pairs = [(j, partner(j, slot)) for j in range(HEADS)]
        landed[slot] = lax.ppermute(after(messages[slot], *before), "patch", pairs)
    return landed


def body(queries, keys, values, grad_out, gain_q, gain_k):
    arrays = (queries, keys, values, grad_out)
    shape = queries.shape
    index = lax.axis_index("patch").reshape(1)
    first, second = (exchange(pack(arrays, c, 1)) for c in range(2))
    leaving, terms = attend(index, first, gain_q, gain_k, False)
    first = exchange(leaving.reshape(HEADS, *leaving.shape[2:]))
    own, other, more = attend(index, second, gain_q, gain_k, True)
    gain_grads = totals_of(jnp.sum(terms + more, axis=0))[-1]
    second = send(compose(index, own, swap(other)), gain_grads)
    grads = unpack_whole(first, 0, 1, shape, ())
    grads = unpack(index, second, 1, shape, grads)
    return (*grads, gain_grads.reshape(2, 1, DEPTH))


def solution(mesh):
    wide = P("clip", "frame", "patch", None)
    gain = P("patch", None)
    return jax.shard_map(
        body,
        mesh=mesh,
        in_specs=(wide, wide, wide, wide, gain, gain),
        out_specs=(wide, wide, wide, P(None, "patch", None)),
        check_vma=False,
    )
```

```python
import math

import jax
import jax.numpy as jnp
from jax import lax
from jax.experimental import pallas as pl
from jax.experimental.pallas import tpu as pltpu
from jax.sharding import PartitionSpec as P

EPS = 1e-06
HEADS = 16
DEPTH = 128
BLOCK = 256
VMEM_LIMIT = 63 * 1024 * 1024
WINDOW = 5
CHIPS = HEADS // 2
ORDER = (1, 7, 2, 6, 3, 5, 4)
F32 = jnp.float32
BF16 = jnp.bfloat16


def partner(index, slot):
    z, core = index // 2, index % 2
    return (z + (slot if core == 0 else CHIPS - slot)) % CHIPS * 2 + core


def chip_of(index, slot):
    return ((index >> 1) + jnp.where((index & 1) == 0, slot, CHIPS - slot)) & (CHIPS - 1)


def source_of(index, slot):
    return chip_of(index, CHIPS - slot)


def pack_kernel(q_ref, k_ref, v_ref, g_ref, out_ref):
    for a, ref in enumerate((q_ref, k_ref, v_ref, g_ref)):
        for h in range(HEADS):
            out_ref[h, a, 0] = ref[0, 0, :, h * DEPTH : (h + 1) * DEPTH]


def pack(arrays, first, clips):
    _, frames, rows, width = arrays[0].shape
    items = clips * frames
    spec = pl.BlockSpec((1, 1, rows, width), lambda i: (first + i // frames, i % frames, 0, 0))
    return pl.pallas_call(
        pack_kernel,
        grid=(items,),
        in_specs=[spec] * 4,
        out_specs=pl.BlockSpec((HEADS, 4, 1, rows, DEPTH), lambda i: (0, 0, i, 0, 0)),
        out_shape=jax.ShapeDtypeStruct((HEADS, 4, items, rows, DEPTH), BF16),
        compiler_params=pltpu.CompilerParams(vmem_limit_bytes=VMEM_LIMIT),
        name="pack",
    )(*arrays)


def compose(index, own, other):
    _, kinds, items, rows, _ = own.shape

    def kernel(index_ref, own_ref, other_ref, *messages):
        for s in range(CHIPS):
            chip = chip_of(index_ref[0], s)
            messages[s][0] = own_ref[chip]
            messages[s][1] = other_ref[chip]

    return pl.pallas_call(
        kernel,
        grid_spec=pltpu.PrefetchScalarGridSpec(
            num_scalar_prefetch=1,
            grid=(items,),
            in_specs=[pl.BlockSpec((CHIPS, kinds, 1, rows, DEPTH), lambda i, _: (0, 0, i, 0, 0))] * 2,
            out_specs=[pl.BlockSpec((2, kinds, 1, rows, DEPTH), lambda i, _: (0, 0, i, 0, 0))] * CHIPS,
        ),
        out_shape=[jax.ShapeDtypeStruct((2, kinds, items, rows, DEPTH), BF16)] * CHIPS,
        compiler_params=pltpu.CompilerParams(vmem_limit_bytes=VMEM_LIMIT),
        name="compose",
    )(index, own, other)


def unpack_kernel(in_ref, *refs):
    for a, ref in enumerate(refs[-3:]):
        for h in range(HEADS):
            ref[0, 0, :, h * DEPTH : (h + 1) * DEPTH] = in_ref[h, a, 0]


def unpack_whole(arrived, first, clips, shape, earlier):
    _, frames, rows, width = shape
    items = clips * frames
    spec = pl.BlockSpec((1, 1, rows, width), lambda i: (first + i // frames, i % frames, 0, 0))
    return pl.pallas_call(
        unpack_kernel,
        grid=(items,),
        in_specs=[pl.BlockSpec((HEADS, 3, 1, rows, DEPTH), lambda i: (0, 0, i, 0, 0))]
        + [pl.BlockSpec(memory_space=pl.ANY)] * len(earlier),
        out_specs=[spec] * 3,
        out_shape=[jax.ShapeDtypeStruct(shape, BF16)] * 3,
        input_output_aliases={1 + i: i for i in range(len(earlier))},
        compiler_params=pltpu.CompilerParams(vmem_limit_bytes=VMEM_LIMIT),
        name="unpack_whole",
    )(arrived, *earlier)


def unpack(index, messages, clip, shape, earlier):
    _, frames, rows, width = shape

    def kernel(index_ref, *refs):
        for s in range(CHIPS):
            chip = source_of(index_ref[0], s)
            for hh in range(2):
                head = 2 * chip + ((index_ref[0] & 1) ^ hh)
                at = pl.ds(pl.multiple_of(head * DEPTH, DEPTH), DEPTH)
                for a in range(3):
                    refs[-3 + a][0, 0, :, at] = refs[s][hh, a, 0]

    return pl.pallas_call(
        kernel,
        grid_spec=pltpu.PrefetchScalarGridSpec(
            num_scalar_prefetch=1,
            grid=(frames,),
            in_specs=[pl.BlockSpec((2, 3, 1, rows, DEPTH), lambda i, _: (0, 0, i, 0, 0))] * CHIPS
            + [pl.BlockSpec(memory_space=pl.ANY)] * len(earlier),
            out_specs=[pl.BlockSpec((1, 1, rows, width), lambda i, _: (clip, i, 0, 0))] * 3,
        ),
        out_shape=[jax.ShapeDtypeStruct(shape, BF16)] * 3,
        input_output_aliases={1 + CHIPS + i: i for i in range(len(earlier))},
        compiler_params=pltpu.CompilerParams(vmem_limit_bytes=VMEM_LIMIT),
        name="unpack",
    )(index, *messages, *earlier)


def normalize(raw, gain):
    wide = raw.astype(F32)
    scale = lax.rsqrt(jnp.mean(wide * wide, axis=-1, keepdims=True) + EPS)
    unit = wide * scale
    return unit, scale, (unit * gain).astype(BF16)


def restore(grad_norm, unit, scale, gain):
    grad_unit = grad_norm * gain
    along = jnp.mean(grad_unit * unit, axis=-1, keepdims=True)
    return (scale * (grad_unit - unit * along)).astype(BF16), grad_norm * unit


def dot(a, b, dims):
    return lax.dot_general(a, b, (dims, ((), ())), preferred_element_type=F32)


def attend_kernel(index_ref, in_ref, gain_q_ref, gain_k_ref, *refs):
    *outs, gains_ref, gv_ref, gk_ref = refs
    sources, _, _, rows, depth = in_ref.shape
    total = sources * rows
    inverse = 1.0 / math.sqrt(depth)
    gain_q = gain_q_ref[...]
    gain_k = gain_k_ref[...]

    low = (index_ref[0] & 1) == 0

    def whole(a):
        return in_ref[:, a, 0].reshape(total, depth)

    def put(first, a, value):
        value = value.reshape(-1, 2, rows, depth)
        chips = pl.ds(first, value.shape[0])
        if len(outs) == 1:
            outs[0][chips, :, a, 0] = value
        else:
            outs[0][chips, a, 0] = jnp.where(low, value[:, 0], value[:, 1])
            outs[1][chips, a, 0] = jnp.where(low, value[:, 1], value[:, 0])

    k_unit, k_scale, k_norm = normalize(whole(1), gain_k)
    values = whole(2)
    k_turned = k_norm.T
    each = BLOCK // rows
    term_q = jnp.zeros((1, depth), F32)
    for b in range(total // BLOCK):
        part = pl.ds(b * each, each)
        q_unit, q_scale, q_norm = normalize(in_ref[part, 0, 0].reshape(BLOCK, depth), gain_q)
        grad_out = in_ref[part, 3, 0].reshape(BLOCK, depth)
        scores = dot(k_norm, q_norm, ((1,), (1,)))
        top = jnp.max(scores, axis=0, keepdims=True)
        expo = jnp.exp2((scores - top) * (inverse * math.log2(math.e)))
        prob = expo * (1.0 / jnp.sum(expo, axis=0, keepdims=True))
        dprob = dot(values, grad_out, ((1,), (1,)))
        delta = jnp.sum(prob * dprob, axis=0, keepdims=True)
        dscore = (prob * (dprob - delta)).astype(BF16)
        grad_v = dot(prob.astype(BF16), grad_out, ((1,), (0,)))
        grad_k = dot(dscore, q_norm, ((1,), (0,)))
        if b == 0:
            gv_ref[...] = grad_v
            gk_ref[...] = grad_k
        else:
            gv_ref[...] += grad_v
            gk_ref[...] += grad_k
        grad_qn = dot(k_turned, dscore, ((1,), (0,))).T * inverse
        grad_q, term = restore(grad_qn, q_unit, q_scale, gain_q)
        put(b * each // 2, 0, grad_q)
        term_q += jnp.sum(term, axis=0, keepdims=True)
    grad_k, term = restore(gk_ref[...] * inverse, k_unit, k_scale, gain_k)
    put(0, 1, grad_k)
    put(0, 2, gv_ref[...].astype(BF16))
    gains_ref[0, 0:1] = term_q
    gains_ref[0, 1:2] = jnp.sum(term, axis=0, keepdims=True)


def attend(index, arrived, gain_q, gain_k, apart):
    sources, _, items, rows, depth = arrived.shape
    total = sources * rows
    gain = pl.BlockSpec((1, depth), lambda i, _: (0, 0))
    if apart:
        outs = [(CHIPS, 3, items, rows, depth)] * 2
        specs = [pl.BlockSpec((CHIPS, 3, 1, rows, depth), lambda i, _: (0, 0, i, 0, 0))] * 2
    else:
        outs = [(CHIPS, 2, 3, items, rows, depth)]
        specs = [pl.BlockSpec((CHIPS, 2, 3, 1, rows, depth), lambda i, _: (0, 0, 0, i, 0, 0))]
    return pl.pallas_call(
        attend_kernel,
        grid_spec=pltpu.PrefetchScalarGridSpec(
            num_scalar_prefetch=1,
            grid=(items,),
            in_specs=[
                pl.BlockSpec((sources, 4, 1, rows, depth), lambda i, _: (0, 0, i, 0, 0)),
                gain,
                gain,
            ],
            out_specs=specs + [pl.BlockSpec((1, 2, depth), lambda i, _: (i, 0, 0))],
            scratch_shapes=[pltpu.VMEM((total, depth), F32)] * 2,
        ),
        out_shape=[jax.ShapeDtypeStruct(shape, BF16) for shape in outs]
        + [jax.ShapeDtypeStruct((items, 2, depth), F32)],
        compiler_params=pltpu.CompilerParams(vmem_limit_bytes=VMEM_LIMIT),
        cost_estimate=pl.CostEstimate(
            flops=items * 10 * total * total * depth,
            bytes_accessed=items * total * depth * 14,
            transcendentals=items * total * total,
        ),
        name="attend",
    )(index, arrived, gain_q, gain_k)


def totals_of(x):
    steps = []
    for axis in ("clip", "frame"):
        size, step = lax.axis_size(axis), 1
        while step < size:
            x = x + lax.ppermute(x, axis, [(i, i ^ step) for i in range(size)])
            steps.append(x)
            step *= 2
    return steps


def after(x, *earlier):
    return lax.optimization_barrier((x, *earlier))[0] if earlier else x


def swap(x):
    return lax.ppermute(x, "patch", [(i, i ^ 1) for i in range(HEADS)])


def exchange(x):
    return lax.all_to_all(x, "patch", split_axis=0, concat_axis=0, tiled=True)


def send(messages, earlier):
    landed = list(messages)
    for i, slot in enumerate(ORDER):
        before = (landed[ORDER[i - WINDOW]],) if i >= WINDOW else (earlier,)
        pairs = [(j, partner(j, slot)) for j in range(HEADS)]
        landed[slot] = lax.ppermute(after(messages[slot], *before), "patch", pairs)
    return landed


def body(queries, keys, values, grad_out, gain_q, gain_k):
    arrays = (queries, keys, values, grad_out)
    shape = queries.shape
    index = lax.axis_index("patch").reshape(1)
    first, second = (exchange(pack(arrays, c, 1)) for c in range(2))
    leaving, terms = attend(index, first, gain_q, gain_k, False)
    first = exchange(leaving.reshape(HEADS, *leaving.shape[2:]))
    own, other, more = attend(index, second, gain_q, gain_k, True)
    gain_grads = totals_of(jnp.sum(terms + more, axis=0))[-1]
    second = send(compose(index, own, swap(other)), gain_grads)
    grads = unpack_whole(first, 0, 1, shape, ())
    grads = unpack(index, second, 1, shape, grads)
    return (*grads, gain_grads.reshape(2, 1, DEPTH))


def solution(mesh):
    wide = P("clip", "frame", "patch", None)
    gain = P("patch", None)
    return jax.shard_map(
        body,
        mesh=mesh,
        in_specs=(wide, wide, wide, wide, gain, gain),
        out_specs=(wide, wide, wide, P(None, "patch", None)),
        check_vma=False,
    )
```
